256 devices in a mesh: outer: 16 (over z_lo, y, core), inner: 16 (over z_hi, x).
Axes of the slice: x: 4, y: 4, z: 8 (z_hi: 4, z_lo: 2; z = z_hi * 2 + z_lo), core: 2. Of those that a mesh axis runs over, the one named last changes fastest.
Arguments:
- queries: bfloat16 [8192, 2048], P(('outer', 'inner')), may hold values from -9 to 9
- keys: bfloat16 [8192, 2048], P(('outer', 'inner')), may hold values from -9 to 9
- values: bfloat16 [8192, 2048], P(('outer', 'inner')), may hold values from -6 to 6
- outputs: bfloat16 [8192, 2048], P(('outer', 'inner')), may hold values from -2 to 2
- out_grads: bfloat16 [8192, 2048], P(('outer', 'inner')), may hold values from -6 to 6
Outputs:
- query_grads: bfloat16 [8192, 2048], P(('outer', 'inner'))
- key_grads: bfloat16 [8192, 2048], P(('outer', 'inner'))
- value_grads: bfloat16 [8192, 2048], P(('outer', 'inner'))
The draws below stay inside these ranges and needn't reach their ends.
All inputs are finite; a program needn't handle non-finite values.
Results may differ from the reference program's by a relative error of at most 0.0049.
Values may be sent and summed in bfloat16 or wider, within the bound.
A program may use at most 64 MiB of HBM per device.

```python
import math
import jax
import jax.numpy as jnp
from jax import lax

HEADS = 16
HEAD_DIM = 128
TOKENS = 8192


def draw_queries(key, part):
    key = jax.random.fold_in(key, 11)
    full_shape = (TOKENS, HEADS, HEAD_DIM)
    drawn = jnp.clip(2.0 * jax.random.normal(key, full_shape), -8.0, 8.0)
    return drawn.reshape(TOKENS, HEADS * HEAD_DIM).astype(jnp.bfloat16)


def draw_keys(key, part):
    key = jax.random.fold_in(key, 23)
    full_shape = (TOKENS, HEADS, HEAD_DIM)
    drawn = jnp.clip(jax.random.normal(key, full_shape), -6.0, 6.0)
    return drawn.reshape(TOKENS, HEADS * HEAD_DIM).astype(jnp.bfloat16)


def block_scale(key, shape, shards, least, largest):
    level, own = 1.0, jax.random.fold_in(key, 6)
    for dim, shards_of in shards:
        heights = jnp.exp(jax.random.uniform(jax.random.fold_in(own, dim), (shards_of,), jnp.float32, least / len(shards), largest / len(shards)))
        level = level * jnp.repeat(heights, shape[dim] // shards_of).reshape([-1 if axis == dim else 1 for axis in range(len(shape))])
    return level


def gaussian(stream_key, extent, deviation, most, cuts=(), kind=jnp.bfloat16):
    gain = block_scale(stream_key, extent, cuts, -0.22, 0.18) if cuts else 1.0
    values = jax.random.normal(stream_key, extent, jnp.float32) * deviation * gain
    return jnp.minimum(jnp.maximum(values, -most), most).astype(kind)


def setup_inputs(seed: int = 0) -> dict:
    splits = jax.random.split(jax.random.key(seed), 6)
    return {
        "queries": draw_queries(jax.random.fold_in(splits[5], 71), 0),
        "keys": draw_keys(jax.random.fold_in(splits[5], 71), 0),
        "values": gaussian(splits[2], (TOKENS, HEADS * HEAD_DIM), 1.0, 6.0, ((0, 256),)),
        "outputs": gaussian(splits[3], (TOKENS, HEADS * HEAD_DIM), 0.3, 2.0, ((0, 256),)),
        "out_grads": gaussian(splits[4], (TOKENS, HEADS * HEAD_DIM), 1.0, 6.0, ((0, 256),)),
    }


def reference(queries, keys, values, outputs, out_grads):
    softmax_scale = HEAD_DIM ** -0.5
    block_rows = math.gcd(512, TOKENS)
    count_blocks = TOKENS // block_rows

    def by_head(array):
        return array.reshape(TOKENS, HEADS, HEAD_DIM).transpose(1, 0, 2)

    def per_head(items):
        query_rows, key_rows, value_rows, output_rows, grad_rows = items
        row_delta = jnp.sum(grad_rows.astype(jnp.float32) * output_rows.astype(jnp.float32), axis=1)
        query_blocks = query_rows.reshape(count_blocks, block_rows, HEAD_DIM)
        grad_blocks = grad_rows.reshape(count_blocks, block_rows, HEAD_DIM)

        def stats(query_block):
            scores = jnp.dot(query_block, key_rows.T, preferred_element_type=jnp.float32) * softmax_scale
            top_score = jnp.max(scores, axis=1)
            return top_score + jnp.log(jnp.sum(jnp.exp(scores - top_score[:, None]), axis=1))

        log_norm = lax.map(stats, query_blocks)

        def grad_step(running, items_block):
            key_acc, value_acc = running
            query_block, grad_block, norm_block, delta_block = items_block
            scores = jnp.dot(query_block, key_rows.T, preferred_element_type=jnp.float32) * softmax_scale
            probs = jnp.exp(scores - norm_block[:, None])
            prob_half = probs.astype(jnp.bfloat16)
            value_acc = value_acc + jnp.dot(prob_half.T, grad_block, preferred_element_type=jnp.float32)
            prob_grad = jnp.dot(grad_block, value_rows.T, preferred_element_type=jnp.float32)
            score_half = (probs * (prob_grad - delta_block[:, None]) * softmax_scale).astype(jnp.bfloat16)
            query_part = jnp.dot(score_half, key_rows, preferred_element_type=jnp.float32).astype(jnp.bfloat16)
            key_acc = key_acc + jnp.dot(score_half.T, query_block, preferred_element_type=jnp.float32)
            return (key_acc, value_acc), query_part

        zeros_init = jnp.zeros((TOKENS, HEAD_DIM), jnp.float32)
        (key_acc, value_acc), query_parts = lax.scan(
            grad_step, (zeros_init, zeros_init),
            (query_blocks, grad_blocks, log_norm, row_delta.reshape(count_blocks, block_rows)))
        return (query_parts.reshape(TOKENS, HEAD_DIM), key_acc.astype(jnp.bfloat16), value_acc.astype(jnp.bfloat16))

    query_out, key_out, value_out = lax.map(
        per_head, (by_head(queries), by_head(keys), by_head(values), by_head(outputs), by_head(out_grads)))

    def back(array):
        return array.transpose(1, 0, 2).reshape(TOKENS, HEADS * HEAD_DIM)

    return (back(query_out), back(key_out), back(value_out))
```

```python
import functools

import jax
import jax.numpy as jnp
import numpy as np
from jax import lax
from jax.experimental import pallas as pl
from jax.experimental.pallas import tpu as pltpu
from jax.sharding import PartitionSpec as P

HEAD_DIM = 128
MESH = pl.DeviceIdType.MESH
NT = (((1,), (1,)), ((), ()))
NN = (((1,), (0,)), ((), ()))
LOG2E = float(np.log2(np.e))


def dot(a, b, dims):
    return lax.dot_general(a, b, dims, preferred_element_type=jnp.float32)


def kernel(
    cfg,
    q_in, k_in, v_in, o_in, g_in,
    dq_out, dk_out, dv_out,
    qg, kg, vg, gg, kt, e_s, m_s, l_s, f_s,
    own_o, own_g, d_stage, d_slot, d_all, st, st_in, dqt, dkv, dkv_in, dqb, dq_in, fin,
    in_sem, s1_send, s1_recv, s1_loc,
    kv_send, kv_recv, qg_send, qg_recv, st_send, st_recv,
    r_send, r_recv, dq_send, dq_recv, out_send, out_recv, out_loc,
):
    H, NX, NY, T, TK = cfg
    NZH = H // NX
    D = HEAD_DIM
    B = H * T
    HB = B // 2
    NQ = 4 * B
    scale = D ** (-0.5)
    c_log = scale * LOG2E
    chunks = B // TK

    o = lax.axis_index("outer")
    i = lax.axis_index("inner")
    c = lax.rem(o, 2)
    y = lax.rem(lax.div(o, 2), NY)
    zl = lax.div(o, 2 * NY)
    x = lax.rem(i, NX)
    zh = lax.div(i, NX)

    def dev(zl_, y_, c_, zh_, x_):
        return ((zl_ * NY + y_) * 2 + c_, zh_ * NX + x_)

    def there(r):
        d, dx = r // NX, r % NX
        zl_ = 1 - zl if 2 * d == NZH else zl
        return dev(zl_, y, c, lax.rem(zh + d, NZH), lax.rem(x + dx, NX))

    def back(r):
        d, dx = r // NX, r % NX
        zl_ = 1 - zl if 2 * d == NZH else zl
        return dev(zl_, y, c, lax.rem(zh + NZH - d, NZH), lax.rem(x + NX - dx, NX))

    sib = dev(zl, y, 1 - c, zh, x)
    zpart = dev(1 - zl, y, c, zh, x)

    def ring(t):
        return dev(zl, lax.rem(y + t, NY), c, zh, x)

    def remote(src, dst, ssem, rsem, device):
        return pltpu.make_async_remote_copy(
            src_ref=src, dst_ref=dst, send_sem=ssem, recv_sem=rsem, device_id=device, device_id_type=MESH
        )

    def wait_for(ref, sem):
        pltpu.make_async_copy(ref, ref, sem).wait()

    def cols(h):
        return pl.ds(pl.multiple_of(h * D, D), D)

    def hops(r):
        d, dx = r // NX, r % NX
        dz = min(d, NZH - d) * 2
        return -(dz + min(dx, NX - dx))

    order = sorted(range(1, H), key=hops)

    cp_g = pltpu.make_async_copy(g_in, own_g, in_sem.at[0])
    cp_o = pltpu.make_async_copy(o_in, own_o, in_sem.at[1])
    cp_g.start()
    cp_o.start()

    barrier = pltpu.get_barrier_semaphore()
    partners = [there(r) for r in order] + [ring(1), ring(2), ring(3), sib, zpart]
    for p in partners:
        pl.semaphore_signal(barrier, inc=1, device_id=p, device_id_type=MESH)
    pl.semaphore_wait(barrier, len(partners))

    s1 = ((k_in, kg), (q_in, qg), (v_in, vg), (g_in, gg))
    for pair in ((0, 1), (2, 3)):
        for r in order:
            for a in pair:
                src, dst = s1[a]
                to = there(r)
                remote(
                    src.at[:, cols(to[1])], dst.at[pl.ds(r * T, T), :], s1_send.at[a], s1_recv.at[a], to
                ).start()
        for a in pair:
            src, dst = s1[a]
            pltpu.make_async_copy(src.at[:, cols(i)], dst.at[pl.ds(0, T), :], s1_loc.at[a]).start()

    cp_g.wait()
    cp_o.wait()
    prod = own_g[...].astype(jnp.float32) * own_o[...].astype(jnp.float32)
    prod4 = jnp.concatenate([prod] * 4, axis=0)
    pick = (
        lax.broadcasted_iota(jnp.int32, (H, H * D), 0) == lax.broadcasted_iota(jnp.int32, (H, H * D), 1) // D
    ).astype(jnp.float32)
    delta = lax.dot_general(
        pick, prod4, NT, precision=lax.Precision.HIGHEST, preferred_element_type=jnp.float32
    )
    for h in range(H):
        d_stage[h] = delta[h : h + 1, :]
    for r in order:
        to = there(r)
        remote(d_stage.at[to[1]], d_slot.at[r], s1_send.at[4], s1_recv.at[4], to).start()
    d_slot[0] = d_stage[i]

    def arrived(a):
        dst = s1[a][1]
        wait_for(dst.at[pl.ds(0, T), :], s1_loc.at[a])
        wait_for(dst.at[pl.ds(T, B - T), :], s1_recv.at[a])

    def rows(s):
        return pl.ds(s * B, B)

    def kv_first(a, ref):
        remote(ref.at[rows(0), :], ref.at[rows(2), :], kv_send.at[a, 1], kv_recv.at[a, 1], zpart).start()
        remote(ref.at[rows(0), :], ref.at[rows(1), :], kv_send.at[a, 0], kv_recv.at[a, 0], sib).start()

    def kv_forward(a, ref):
        wait_for(ref.at[rows(2), :], kv_recv.at[a, 1])
        remote(ref.at[rows(2), :], ref.at[rows(3), :], kv_send.at[a, 2], kv_recv.at[a, 2], sib).start()

    def q_first(a, ref):
        remote(ref.at[rows(0), :], ref.at[rows(1), :], qg_send.at[a, 0], qg_recv.at[a, 0], ring(1)).start()
        remote(ref.at[rows(0), :], ref.at[rows(3), :], qg_send.at[a, 1], qg_recv.at[a, 1], ring(3)).start()

    def q_forward(a, ref):
        wait_for(ref.at[rows(1), :], qg_recv.at[a, 0])
        remote(
            ref.at[pl.ds(B, HB), :], ref.at[pl.ds(2 * B, HB), :], qg_send.at[a, 2], qg_recv.at[a, 2], ring(1)
        ).start()
        wait_for(ref.at[rows(3), :], qg_recv.at[a, 1])
        remote(
            ref.at[pl.ds(3 * B + HB, HB), :],
            ref.at[pl.ds(2 * B + HB, HB), :],
            qg_send.at[a, 3],
            qg_recv.at[a, 3],
            ring(3),
        ).start()

    def q_last(a, ref):
        wait_for(ref.at[pl.ds(2 * B, HB), :], qg_recv.at[a, 2])
        wait_for(ref.at[pl.ds(2 * B + HB, HB), :], qg_recv.at[a, 3])

    def stats(qs, first, count):
        qv = qg[rows(qs), :]

        def step(kc, carry):
            ks = pl.ds(pl.multiple_of(kc * TK, TK), TK)
            s = dot(kg[ks, :], qv, NT)
            m = jnp.max(s, axis=0, keepdims=True) * c_log
            e = jnp.exp2(s * c_log - m)
            e_s[ks, rows(qs)] = e
            m_s[pl.ds(kc, 1), rows(qs)] = m
            l_s[pl.ds(kc, 1), rows(qs)] = jnp.sum(e, axis=0, keepdims=True)
            return carry

        lax.fori_loop(first * chunks, (first + count) * chunks, step, 0)

    arrived(0)
    kv_first(0, kg)
    arrived(1)
    q_first(0, qg)
    stats(0, 0, 1)
    wait_for(kg.at[rows(1), :], kv_recv.at[0, 0])
    stats(0, 1, 1)
    kv_forward(0, kg)
    q_forward(0, qg)
    arrived(2)
    kv_first(1, vg)
    arrived(3)
    q_first(1, gg)
    stats(0, 2, 1)
    stats(1, 0, 3)
    stats(3, 0, 3)
    wait_for(kg.at[rows(3), :], kv_recv.at[0, 2])
    stats(0, 3, 1)
    stats(1, 3, 1)
    stats(3, 3, 1)
    kv_forward(1, vg)
    q_forward(1, gg)
    q_last(0, qg)
    stats(2, 0, 4)

    wait_for(d_slot.at[pl.ds(1, H - 1)], s1_recv.at[4])
    lane = lax.broadcasted_iota(jnp.int32, (1, 128), 1) // T
    own_delta = jnp.concatenate(
        [
            sum(jnp.where(lane == j, d_slot[4 * g + j], 0.0) for j in range(4))
            for g in range(H // 4)
        ],
        axis=1,
    )
    for s in range(4):
        m = m_s[:, rows(s)]
        top = jnp.max(m, axis=0, keepdims=True)
        total = jnp.sum(l_s[:, rows(s)] * jnp.exp2(m - top), axis=0, keepdims=True)
        st[pl.ds(s, 1), :] = top + jnp.log2(total)
    st[pl.ds(4, 1), :] = own_delta
    st[pl.ds(5, 3), :] = jnp.zeros((3, B), jnp.float32)
    for t in (1, 2, 3):
        remote(st, st_in.at[t - 1], st_send.at[t - 1], st_recv.at[t - 1], ring(t)).start()
    for s in range(4):
        kt[:, rows(s)] = kg[rows(s), :].T
    for t in (1, 2, 3):
        wait_for(st_in.at[t - 1], st_recv.at[t - 1])
    for s in range(4):
        parts = [st[pl.ds(s, 1), :]] + [st_in[t - 1, pl.ds((s - t) % 4, 1), :] for t in (1, 2, 3)]
        top = functools.reduce(jnp.maximum, parts)
        norm = top + jnp.log2(sum(jnp.exp2(p - top) for p in parts))
        f_s[:, rows(s)] = jnp.exp2(m_s[:, rows(s)] - norm)
        d_all[pl.ds(0, 1), rows(s)] = st[pl.ds(4, 1), :] if s == 0 else st_in[s - 1, pl.ds(4, 1), :]

    wait_for(vg.at[rows(1), :], kv_recv.at[1, 0])
    wait_for(vg.at[rows(3), :], kv_recv.at[1, 2])
    q_last(1, gg)

    def grads(s, first):
        v = vg[rows(s), :]
        ktv = kt[:, rows(s)]
        dk = dv = None
        for qs in range(4):
            g = gg[rows(qs), :]
            q = qg[rows(qs), :]
            dp = dot(v, g, NT)
            p = jnp.concatenate(
                [
                    e_s[pl.ds(s * B + j * TK, TK), rows(qs)] * f_s[pl.ds(s * chunks + j, 1), rows(qs)]
                    for j in range(chunks)
                ],
                axis=0,
            )
            ds = (p * (dp - d_all[pl.ds(0, 1), rows(qs)])).astype(jnp.bfloat16)
            dv_part = dot(p.astype(jnp.bfloat16), g, NN)
            dk_part = dot(ds, q, NN)
            dv = dv_part if dv is None else dv + dv_part
            dk = dk_part if dk is None else dk + dk_part
            dq = dot(ktv, ds, NN)
            dqt[:, rows(qs)] = dq if first else dqt[:, rows(qs)] + dq
        return dk * scale, dv

    def add_in(pair, slot):
        return pair[0] + dkv_in[slot, 0].astype(jnp.float32), pair[1] + dkv_in[slot, 1].astype(jnp.float32)

    def send_pair(pair, slot, device):
        dkv[slot, 0] = pair[0].astype(jnp.bfloat16)
        dkv[slot, 1] = pair[1].astype(jnp.bfloat16)
        remote(dkv.at[slot], dkv_in.at[slot], r_send.at[slot], r_recv.at[slot], device).start()

    send_pair(grads(3, True), 0, sib)
    pair = grads(2, False)
    wait_for(dkv_in.at[0], r_recv.at[0])
    send_pair(add_in(pair, 0), 1, zpart)
    send_pair(grads(1, False), 2, sib)
    pair = grads(0, False)
    for s in (2, 1, 3):
        dqb[s - 1] = (dqt[:, rows(s)] * scale).T.astype(jnp.bfloat16)
        remote(dqb.at[s - 1], dq_in.at[s - 1], dq_send.at[s - 1], dq_recv.at[s - 1], ring(4 - s)).start()
    wait_for(dkv_in.at[1], r_recv.at[1])
    wait_for(dkv_in.at[2], r_recv.at[2])
    pair = add_in(add_in(pair, 1), 2)
    fin[1] = pair[0].astype(jnp.bfloat16)
    fin[2] = pair[1].astype(jnp.bfloat16)

    outs = (dq_out, dk_out, dv_out)

    def send_back(a):
        for r in order:
            remote(
                fin.at[a, pl.ds(r * T, T), :], outs[a].at[:, cols(i)], out_send.at[a], out_recv.at[a], back(r)
            ).start()
        pltpu.make_async_copy(fin.at[a, pl.ds(0, T), :], outs[a].at[:, cols(i)], out_loc.at[a]).start()

    send_back(1)
    send_back(2)
    dq = (dqt[:, rows(0)] * scale).T
    for s in (1, 3, 2):
        wait_for(dq_in.at[s - 1], dq_recv.at[s - 1])
        dq = dq + dq_in[s - 1].astype(jnp.float32)
    fin[0] = dq.astype(jnp.bfloat16)
    send_back(0)

    for a in range(4):
        wait_for(qg.at[pl.ds(T, B - T), :], s1_send.at[a])
    wait_for(d_slot.at[pl.ds(1, H - 1)], s1_send.at[4])
    for a in range(2):
        for j in range(3):
            wait_for(kg.at[rows(0), :], kv_send.at[a, j])
        for j in range(2):
            wait_for(qg.at[rows(0), :], qg_send.at[a, j])
            wait_for(qg.at[pl.ds(0, HB), :], qg_send.at[a, 2 + j])
    for t in range(3):
        wait_for(st, st_send.at[t])
        wait_for(dkv.at[t], r_send.at[t])
        wait_for(dqb.at[t], dq_send.at[t])
    for a in (1, 2, 0):
        wait_for(fin.at[a, pl.ds(T, B - T), :], out_send.at[a])
        wait_for(fin.at[a, pl.ds(0, T), :], out_loc.at[a])
        wait_for(fin.at[a, pl.ds(T, B - T), :], out_recv.at[a])


def attention_backward(nx, outer, inner, queries, keys, values, outputs, out_grads):
    T, W = queries.shape
    D = HEAD_DIM
    H = inner
    B = H * T
    NQ = 4 * B
    TK = min(256, B)
    bf, f32 = jnp.bfloat16, jnp.float32
    dma = pltpu.SemaphoreType.DMA
    vm = pltpu.VMEM
    any_spec = pl.BlockSpec(memory_space=pl.ANY)
    return pl.pallas_call(
        functools.partial(kernel, (H, nx, outer // 4, T, TK)),
        out_shape=[jax.ShapeDtypeStruct((T, W), bf)] * 3,
        in_specs=[any_spec] * 5,
        out_specs=[any_spec] * 3,
        scratch_shapes=[
            vm((NQ, D), bf), vm((NQ, D), bf), vm((NQ, D), bf), vm((NQ, D), bf),
            vm((D, NQ), bf),
            vm((NQ, NQ), f32),
            vm((NQ // TK, NQ), f32), vm((NQ // TK, NQ), f32), vm((NQ // TK, NQ), f32),
            vm((T, W), bf), vm((T, W), bf),
            vm((H, 1, 128), f32), vm((H, 1, 128), f32),
            vm((8, NQ), f32),
            vm((8, B), f32), vm((3, 8, B), f32),
            vm((D, NQ), f32),
            vm((3, 2, B, D), bf), vm((3, 2, B, D), bf),
            vm((3, B, D), bf), vm((3, B, D), bf),
            vm((3, B, D), bf),
            dma((2,)), dma((5,)), dma((5,)), dma((4,)),
            dma((2, 3)), dma((2, 3)), dma((2, 4)), dma((2, 4)), dma((3,)), dma((3,)),
            dma((3,)), dma((3,)), dma((3,)), dma((3,)), dma((3,)), dma((3,)), dma((3,)),
        ],
        compiler_params=pltpu.CompilerParams(
            collective_id=0, has_side_effects=True, vmem_limit_bytes=48 << 20
        ),
        cost_estimate=pl.CostEstimate(flops=6 * 10**9, bytes_accessed=10**6, transcendentals=4 * 10**6),
    )(queries, keys, values, outputs, out_grads)


def solution(mesh, nx=4):
    spec = P(("outer", "inner"), None)
    return jax.shard_map(
        functools.partial(attention_backward, nx, mesh.shape["outer"], mesh.shape["inner"]),
        mesh=mesh,
        in_specs=(spec,) * 5,
        out_specs=(spec,) * 3,
        check_vma=False,
    )
```

```python
import functools

import jax
import jax.numpy as jnp
import numpy as np
from jax import lax
from jax.experimental import pallas as pl
from jax.experimental.pallas import tpu as pltpu
from jax.sharding import PartitionSpec as P

HEAD_DIM = 128
MESH = pl.DeviceIdType.MESH
NT = (((1,), (1,)), ((), ()))
NN = (((1,), (0,)), ((), ()))
LOG2E = float(np.log2(np.e))
S1_ORDER = (0, 2, 1, 3)
VMEM_LIMIT = 62 << 20
VG_AT = 3


def dot(a, b, dims):
    return lax.dot_general(a, b, dims, preferred_element_type=jnp.float32)


def kernel(
    cfg,
    q_in, k_in, v_in, o_in, g_in,
    dq_out, dk_out, dv_out,
    qg, kg, vg, gg, kt, e_s, m_s, l_s, f_s,
    own_o, own_g, d_stage, d_slot, d_all, st, st_in, dqt, dk_s, dv_s, sib_buf, sib_in, z_buf, z_in, dqb, dq_in, fin,
    in_sem, s1_send, s1_recv, s1_loc, d_send, d_recv,
    kv_send, kv_recv, qg_send, qg_recv, st_send, st_recv,
    sib_send, sib_recv, z_send, z_recv, dq_send, dq_recv, out_send, out_recv, out_loc,
):
    H, NX, NY, T, TK = cfg
    NZ = 2 * (H // NX)
    D = HEAD_DIM
    B = H * T
    G = B // 4
    per = H // 4
    scale = D ** (-0.5)
    c_log = scale * LOG2E
    halves = B // TK

    o = lax.axis_index("outer")
    i = lax.axis_index("inner")
    c = lax.rem(o, 2)
    y = lax.rem(lax.div(o, 2), NY)
    zl = lax.div(o, 2 * NY)
    x = lax.rem(i, NX)
    z = 2 * lax.div(i, NX) + zl
    up = 2 * zl - 1

    def dev(z_, y_, c_, x_):
        return ((lax.rem(z_, 2) * NY + y_) * 2 + c_, lax.div(z_, 2) * NX + x_)

    def along(dz, dx):
        return dev(lax.rem(z + dz + NZ, NZ), y, c, lax.rem(x + dx, NX))

    def there(r):
        g, dx = r // NX, r % NX
        return along((0, -2 * up, up, 3 * up)[g], dx)

    def back(r):
        g, dx = r // NX, r % NX
        return along((0, 2 * up, up, 3 * up)[g], NX - dx)

    sib = dev(z, y, 1 - c, x)
    zpart = dev(z - up, y, c, x)
    diag = dev(z - up, y, 1 - c, x)

    def ring(t):
        return dev(z, lax.rem(y + t, NY), c, x)

    def remote(src, dst, ssem, rsem, device):
        pltpu.make_async_remote_copy(
            src_ref=src, dst_ref=dst, send_sem=ssem, recv_sem=rsem, device_id=device, device_id_type=MESH
        ).start()

    def wait_for(ref, sem):
        pltpu.make_async_copy(ref, ref, sem).wait()

    def cols(h):
        return pl.ds(pl.multiple_of(h * D, D), D)

    cp_g = pltpu.make_async_copy(g_in, own_g, in_sem.at[0])
    cp_o = pltpu.make_async_copy(o_in, own_o, in_sem.at[1])
    cp_g.start()
    cp_o.start()

    barrier = pltpu.get_barrier_semaphore()
    partners = [there(r) for r in range(H - 1, 0, -1)] + [back(NX + dx) for dx in range(NX)]
    partners += [ring(2), ring(1), ring(3), diag, zpart, sib]
    for p in partners:
        pl.semaphore_signal(barrier, inc=1, device_id=p, device_id_type=MESH)

    pl.semaphore_wait(barrier, len(partners))

    PLACE = (3, 1, 2, 0)

    def part(s, g):
        return pl.ds(g * B + PLACE[s] * G, G)

    def group(g):
        return pl.ds(g * B, B)

    s1 = ((k_in, kg), (q_in, qg), (v_in, vg), (g_in, gg))

    def s1_sends(pair):
        for a in pair:
            src, dst = s1[a]
            pltpu.make_async_copy(src.at[:, cols(i)], dst.at[pl.ds(PLACE[0] * G, T), :], s1_loc.at[a]).start()
        for g in S1_ORDER:
            for j in range(per):
                r = g * per + j
                if r == 0:
                    continue
                to = there(r)
                for a in pair:
                    src, dst = s1[a]
                    remote(
                        src.at[:, cols(to[1])],
                        dst.at[pl.ds(g * B + PLACE[0] * G + j * T, T), :],
                        s1_send.at[a],
                        s1_recv.at[a, g],
                        to,
                    )

    s1_sends((0, 1))
    if VG_AT == 0:
        s1_sends((2, 3))

    cp_g.wait()
    cp_o.wait()
    prod = own_g[...].astype(jnp.float32) * own_o[...].astype(jnp.float32)
    prod4 = jnp.concatenate([prod] * 4, axis=0)
    pick = (
        lax.broadcasted_iota(jnp.int32, (H, H * D), 0) == lax.broadcasted_iota(jnp.int32, (H, H * D), 1) // D
    ).astype(jnp.float32)
    delta = lax.dot_general(
        pick, prod4, NT, precision=lax.Precision.HIGHEST, preferred_element_type=jnp.float32
    )
    for h in range(H):
        d_stage[h] = delta[h : h + 1, :]
    d_slot[0] = d_stage[i]
    for r in range(1, H):
        to = there(r)
        remote(d_stage.at[to[1]], d_slot.at[r], d_send, d_recv, to)

    def arrived(a, g):
        dst = s1[a][1]
        if g == 0:
            wait_for(dst.at[pl.ds(PLACE[0] * G, T), :], s1_loc.at[a])
            if G > T:
                wait_for(dst.at[pl.ds(PLACE[0] * G + T, G - T), :], s1_recv.at[a, g])
        else:
            wait_for(dst.at[part(0, g), :], s1_recv.at[a, g])

    def first(n, g):
        kv, qd = (kg, vg)[n], (qg, gg)[n]
        arrived(2 * n, g)
        remote(kv.at[part(0, g), :], kv.at[part(2, g), :], kv_send.at[n, 2, g], kv_recv.at[n, 2, g], zpart)
        remote(kv.at[part(0, g), :], kv.at[part(1, g), :], kv_send.at[n, 1, g], kv_recv.at[n, 1, g], sib)
        arrived(2 * n + 1, g)
        for t in (2, 1, 3):
            remote(qd.at[part(0, g), :], qd.at[part(t, g), :], qg_send.at[n, t - 1, g], qg_recv.at[n, t - 1, g], ring(t))

    def forward(n, g):
        kv = (kg, vg)[n]
        wait_for(kv.at[part(2, g), :], kv_recv.at[n, 2, g])
        remote(kv.at[part(2, g), :], kv.at[part(3, g), :], kv_send.at[n, 0, g], kv_recv.at[n, 0, g], sib)

    def complete(n, g):
        kv, qd = (kg, vg)[n], (qg, gg)[n]
        for t in (1, 3, 2):
            wait_for(qd.at[part(t, g), :], qg_recv.at[n, t - 1, g])
        wait_for(kv.at[part(1, g), :], kv_recv.at[n, 1, g])
        wait_for(kv.at[part(3, g), :], kv_recv.at[n, 0, g])

    def stats(*blocks):
        for gq, gk in blocks:
            for h in range(halves):
                kc = gk * halves + h
                ks = pl.ds(kc * TK, TK)
                s = dot(kg[ks, :], qg[group(gq), :], NT)
                m = jnp.max(s, axis=0, keepdims=True) * c_log
                e = jnp.exp2(s * c_log - m)
                e_s[ks, group(gq)] = e
                m_s[pl.ds(kc, 1), group(gq)] = m
                l_s[pl.ds(kc, 1), group(gq)] = jnp.sum(e, axis=0, keepdims=True)

    lane = lax.broadcasted_iota(jnp.int32, (1, 128), 1) // T

    def stats_send(g):
        m = m_s[:, group(g)]
        top = jnp.max(m, axis=0, keepdims=True)
        total = jnp.sum(l_s[:, group(g)] * jnp.exp2(m - top), axis=0, keepdims=True)
        st[g, :, pl.ds(0, B)] = top + jnp.log2(total)
        st[g, :, pl.ds(B, 128)] = sum(jnp.where(lane == j, d_slot[per * g + j], 0.0) for j in range(per))
        for t in (2, 1, 3):
            remote(st.at[g], st_in.at[t - 1, g], st_send.at[t - 1, g], st_recv.at[t - 1, g], ring(t))

    def lanes(s):
        return pl.ds(PLACE[s] * G, G)

    def stats_take(g):
        for t in (1, 3, 2):
            wait_for(st_in.at[t - 1, g], st_recv.at[t - 1, g])
        for s in range(4):
            parts = [st[g, :, lanes(s)]] + [st_in[t - 1, g, :, lanes((s - t) % 4)] for t in (1, 2, 3)]
            top = functools.reduce(jnp.maximum, parts)
            norm = top + jnp.log2(sum(jnp.exp2(p - top) for p in parts))
            f_s[:, part(s, g)] = jnp.exp2(m_s[:, part(s, g)] - norm)
            delta_rows = st[g, :, pl.ds(B, G)] if s == 0 else st_in[s - 1, g, :, pl.ds(B, G)]
            d_all[pl.ds(0, 1), part(s, g)] = delta_rows

    def transpose_keys(g):
        kt[:, group(g)] = kg[group(g), :].T

    a, b, c3, d = S1_ORDER
    for n, g in enumerate(S1_ORDER):
        first(0, g)
        if n:
            forward(0, S1_ORDER[n - 1])
        if VG_AT == n + 1:
            s1_sends((2, 3))
    complete(0, a)
    stats((a, a))
    forward(0, d)
    complete(0, b)
    stats((a, b), (b, a), (b, b))
    complete(0, c3)
    stats((a, c3), (b, c3), (c3, a), (c3, b), (c3, c3))
    first(1, a)
    complete(0, d)
    wait_for(d_slot.at[pl.ds(1, H - 1)], d_recv)
    stats((a, d), (b, d), (c3, d))
    for g in (a, b, c3):
        stats_send(g)
    first(1, b)
    stats((d, a), (d, b), (d, c3), (d, d))
    stats_send(d)
    first(1, c3)
    forward(1, a)
    first(1, d)
    for g in (b, c3, d):
        forward(1, g)
    for g in range(4):
        transpose_keys(g)
    for g in range(4):
        complete(1, g)

    seen = set()

    def block(gq, gk):
        start_q, start_k = (gq, "q") not in seen, (gk, "k") not in seen
        seen.update(((gq, "q"), (gk, "k")))
        gv = gg[group(gq), :]
        qv = qg[group(gq), :]
        dp = dot(vg[group(gk), :], gv, NT)
        p = jnp.concatenate(
            [
                e_s[pl.ds(gk * B + h * TK, TK), group(gq)] * f_s[pl.ds(gk * halves + h, 1), group(gq)]
                for h in range(halves)
            ],
            axis=0,
        )
        ds = (p * ((dp - d_all[pl.ds(0, 1), group(gq)]) * scale)).astype(jnp.bfloat16)
        dv = dot(p.astype(jnp.bfloat16), gv, NN)
        dk = dot(ds, qv, NN)
        dq = dot(kt[:, group(gk)], ds, NN)
        dv_s[group(gk), :] = dv if start_k else dv_s[group(gk), :] + dv
        dk_s[group(gk), :] = dk if start_k else dk_s[group(gk), :] + dk
        dqt[:, group(gq)] = dq if start_q else dqt[:, group(gq)] + dq

    outs = (dq_out, dk_out, dv_out)

    def send_back(a, g):
        for j in range(per):
            r = g * per + j
            here = fin.at[a, pl.ds(r * T, T), :]
            if r == 0:
                pltpu.make_async_copy(here, outs[a].at[:, cols(i)], out_loc.at[a]).start()
            else:
                remote(here, outs[a].at[:, cols(i)], out_send.at[a], out_recv.at[a], back(r))

    sums = (dk_s, dv_s)

    def rows_of(g, first_row, count):
        return pl.ds(g * B + first_row * G, count * G)

    def to_sib(g):
        for j in range(2):
            sib_buf[g, j] = sums[j][rows_of(g, 0, 2), :].astype(jnp.bfloat16)
        remote(sib_buf.at[g], sib_in.at[g], sib_send.at[g], sib_recv.at[g], sib)

    def to_z(g):
        wait_for(sib_in.at[g], sib_recv.at[g])
        for j in range(2):
            t = sums[j][rows_of(g, 2, 1), :] + sib_in[g, j, pl.ds(0, G)].astype(jnp.float32)
            z_buf[g, j] = t.astype(jnp.bfloat16)
        remote(z_buf.at[g], z_in.at[g], z_send.at[g], z_recv.at[g], zpart)

    def to_owner(g):
        wait_for(z_in.at[g], z_recv.at[g])
        for j in range(2):
            t = sums[j][rows_of(g, 3, 1), :] + sib_in[g, j, pl.ds(G, G)].astype(jnp.float32)
            fin[1 + j, pl.ds(g * G, G), :] = (t + z_in[g, j].astype(jnp.float32)).astype(jnp.bfloat16)
        send_back(1, g)
        send_back(2, g)

    def dq_send_parts(g):
        for s in (2, 1, 3):
            dqb[s - 1, g] = dqt[:, part(s, g)].T.astype(jnp.bfloat16)
            remote(
                dqb.at[s - 1, g], dq_in.at[s - 1, g], dq_send.at[s - 1, g], dq_recv.at[s - 1, g], ring(4 - s)
            )

    def dq_owner(g):
        dq = dqt[:, part(0, g)].T
        for s in (1, 3, 2):
            wait_for(dq_in.at[s - 1, g], dq_recv.at[s - 1, g])
            dq = dq + dq_in[s - 1, g].astype(jnp.float32)
        fin[0, pl.ds(g * G, G), :] = dq.astype(jnp.bfloat16)
        send_back(0, g)

    k1, k2, k3, k4 = (3, 1, 2, 0)
    soon = [g for g in (k1, k2, k3, k4) if g != d] + [d]
    for g in soon:
        stats_take(g)
        block(g, k1)
    to_sib(k1)
    block(k1, k2)
    block(k1, k3)
    to_z(k1)
    block(k1, k4)
    dq_send_parts(k1)
    block(k2, k2)
    block(k3, k2)
    block(k4, k2)
    to_sib(k2)
    block(k2, k3)
    block(k2, k4)
    to_z(k2)
    dq_send_parts(k2)
    to_owner(k1)
    block(k3, k3)
    block(k4, k3)
    to_sib(k3)
    dq_owner(k1)
    block(k3, k4)
    dq_send_parts(k3)
    block(k4, k4)
    to_sib(k4)
    dq_send_parts(k4)
    to_z(k3)
    to_z(k4)
    dq_owner(k2)
    to_owner(k2)
    dq_owner(k3)
    to_owner(k3)
    dq_owner(k4)
    to_owner(k4)

    for a in range(4):
        wait_for(qg.at[pl.ds(T, B - T), :], s1_send.at[a])
    wait_for(d_slot.at[pl.ds(1, H - 1)], d_send)
    for n in range(2):
        for s in range(3):
            for g in range(4):
                wait_for(kg.at[part(0, g), :], kv_send.at[n, s, g])
                wait_for(qg.at[part(0, g), :], qg_send.at[n, s, g])
    for g in range(4):
        for t in range(3):
            wait_for(st.at[g], st_send.at[t, g])
            wait_for(dqb.at[t, g], dq_send.at[t, g])
        wait_for(sib_buf.at[g], sib_send.at[g])
        wait_for(z_buf.at[g], z_send.at[g])
    for a in (1, 2, 0):
        wait_for(fin.at[a, pl.ds(T, B - T), :], out_send.at[a])
        wait_for(fin.at[a, pl.ds(0, T), :], out_loc.at[a])
        wait_for(fin.at[a, pl.ds(T, B - T), :], out_recv.at[a])


def attention_backward(nx, outer, inner, queries, keys, values, outputs, out_grads):
    T, W = queries.shape
    D = HEAD_DIM
    H = inner
    B = H * T
    NQ = 4 * B
    TK = min(256, B)
    bf, f32 = jnp.bfloat16, jnp.float32
    dma = pltpu.SemaphoreType.DMA
    vm = pltpu.VMEM
    hbm = pl.BlockSpec(memory_space=pltpu.HBM)
    return pl.pallas_call(
        functools.partial(kernel, (H, nx, outer // 4, T, TK)),
        out_shape=[jax.ShapeDtypeStruct((T, W), bf)] * 3,
        in_specs=[hbm] * 5,
        out_specs=[hbm] * 3,
        scratch_shapes=[
            vm((NQ, D), bf), vm((NQ, D), bf), vm((NQ, D), bf), vm((NQ, D), bf),
            vm((D, NQ), bf),
            vm((NQ, NQ), f32),
            vm((NQ // TK, NQ), f32), vm((NQ // TK, NQ), f32), vm((NQ // TK, NQ), f32),
            vm((T, W), bf), vm((T, W), bf),
            vm((H, 1, 128), f32), vm((H, 1, 128), f32),
            vm((8, NQ), f32),
            vm((4, 1, B + 128), f32), vm((3, 4, 1, B + 128), f32),
            vm((D, NQ), f32),
            vm((NQ, D), f32), vm((NQ, D), f32),
            vm((4, 2, B // 2, D), bf), vm((4, 2, B // 2, D), bf),
            vm((4, 2, B // 4, D), bf), vm((4, 2, B // 4, D), bf),
            vm((3, 4, B // 4, D), bf), vm((3, 4, B // 4, D), bf),
            vm((3, B, D), bf),
            dma((2,)), dma((4,)), dma((4, 4)), dma((4,)), dma, dma,
            dma((2, 3, 4)), dma((2, 3, 4)), dma((2, 3, 4)), dma((2, 3, 4)), dma((3, 4)), dma((3, 4)),
            dma((4,)), dma((4,)), dma((4,)), dma((4,)), dma((3, 4)), dma((3, 4)), dma((3,)), dma((3,)), dma((3,)),
        ],
        compiler_params=pltpu.CompilerParams(
            collective_id=0, has_side_effects=True, vmem_limit_bytes=VMEM_LIMIT
        ),
        cost_estimate=pl.CostEstimate(flops=6 * 10**9, bytes_accessed=10**6, transcendentals=4 * 10**6),
    )(queries, keys, values, outputs, out_grads)


def solution(mesh, nx=4):
    spec = P(("outer", "inner"), None)
    return jax.shard_map(
        functools.partial(attention_backward, nx, mesh.shape["outer"], mesh.shape["inner"]),
        mesh=mesh,
        in_specs=(spec,) * 5,
        out_specs=(spec,) * 3,
        check_vma=False,
    )
```

```python
import functools

import jax
import jax.numpy as jnp
import numpy as np
from jax import lax
from jax.experimental import pallas as pl
from jax.experimental.pallas import tpu as pltpu
from jax.sharding import PartitionSpec as P

HEAD_DIM = 128
MESH = pl.DeviceIdType.MESH
NT = (((1,), (1,)), ((), ()))
NN = (((1,), (0,)), ((), ()))
LOG2E = float(np.log2(np.e))
S1_ORDER = (0, 2, 1, 3)
VMEM_LIMIT = 62 << 20
VG_AT = 3


def dot(a, b, dims):
    return lax.dot_general(a, b, dims, preferred_element_type=jnp.float32)


def kernel(
    cfg,
    q_in, k_in, v_in, o_in, g_in,
    dq_out, dk_out, dv_out,
    qg, kg, vg, gg, kt, e_s, m_s, l_s, f_s,
    own_o, own_g, d_stage, d_slot, d_all, st, st_in, dqt, dk_s, dv_s, sib_buf, sib_in, z_buf, z_in, dqb, dq_in, fin,
    in_sem, s1_send, s1_recv, s1_loc, d_send, d_recv,
    kv_send, kv_recv, qg_send, qg_recv, st_send, st_recv,
    sib_send, sib_recv, z_send, z_recv, dq_send, dq_recv, out_send, out_recv, out_loc,
):
    H, NX, NY, T, TK = cfg
    NZ = 2 * (H // NX)
    D = HEAD_DIM
    B = H * T
    G = B // 4
    per = H // 4
    scale = D ** (-0.5)
    c_log = scale * LOG2E
    halves = B // TK

    o = lax.axis_index("outer")
    i = lax.axis_index("inner")
    c = lax.rem(o, 2)
    y = lax.rem(lax.div(o, 2), NY)
    zl = lax.div(o, 2 * NY)
    x = lax.rem(i, NX)
    z = 2 * lax.div(i, NX) + zl
    up = 2 * zl - 1

    def dev(z_, y_, c_, x_):
        return ((lax.rem(z_, 2) * NY + y_) * 2 + c_, lax.div(z_, 2) * NX + x_)

    def along(dz, dx):
        return dev(lax.rem(z + dz + NZ, NZ), y, c, lax.rem(x + dx, NX))

    def there(r):
        g, dx = r // NX, r % NX
        return along((0, -2 * up, up, 3 * up)[g], dx)

    def back(r):
        g, dx = r // NX, r % NX
        return along((0, 2 * up, up, 3 * up)[g], NX - dx)

    sib = dev(z, y, 1 - c, x)
    zpart = dev(z - up, y, c, x)
    diag = dev(z - up, y, 1 - c, x)

    def ring(t):
        return dev(z, lax.rem(y + t, NY), c, x)

    def remote(src, dst, ssem, rsem, device):
        pltpu.make_async_remote_copy(
            src_ref=src, dst_ref=dst, send_sem=ssem, recv_sem=rsem, device_id=device, device_id_type=MESH
        ).start()

    def wait_for(ref, sem):
        pltpu.make_async_copy(ref, ref, sem).wait()

    def cols(h):
        return pl.ds(pl.multiple_of(h * D, D), D)

    cp_g = pltpu.make_async_copy(g_in, own_g, in_sem.at[0])
    cp_o = pltpu.make_async_copy(o_in, own_o, in_sem.at[1])
    cp_g.start()
    cp_o.start()

    barrier = pltpu.get_barrier_semaphore()
    partners = [there(r) for r in range(H - 1, 0, -1)] + [back(NX + dx) for dx in range(NX)]
    partners += [ring(2), ring(1), ring(3), diag, zpart, sib]
    for p in partners:
        pl.semaphore_signal(barrier, inc=1, device_id=p, device_id_type=MESH)

    pl.semaphore_wait(barrier, len(partners))

    PLACE = (3, 1, 2, 0)

    def part(s, g):
        return pl.ds(g * B + PLACE[s] * G, G)

    def group(g):
        return pl.ds(g * B, B)

    s1 = ((k_in, kg), (q_in, qg), (v_in, vg), (g_in, gg))

    def s1_sends(pair):
        for a in pair:
            src, dst = s1[a]
            pltpu.make_async_copy(src.at[:, cols(i)], dst.at[pl.ds(PLACE[0] * G, T), :], s1_loc.at[a]).start()
        for g in S1_ORDER:
            for j in range(per):
                r = g * per + j
                if r == 0:
                    continue
                to = there(r)
                for a in pair:
                    src, dst = s1[a]
                    remote(
                        src.at[:, cols(to[1])],
                        dst.at[pl.ds(g * B + PLACE[0] * G + j * T, T), :],
                        s1_send.at[a],
                        s1_recv.at[a, g],
                        to,
                    )

    s1_sends((0, 1))

    cp_g.wait()
    cp_o.wait()
    prod = own_g[...].astype(jnp.float32) * own_o[...].astype(jnp.float32)
    prod4 = jnp.concatenate([prod] * 4, axis=0)
    pick = (
        lax.broadcasted_iota(jnp.int32, (H, H * D), 0) == lax.broadcasted_iota(jnp.int32, (H, H * D), 1) // D
    ).astype(jnp.float32)
    delta = lax.dot_general(
        pick, prod4, NT, precision=lax.Precision.HIGHEST, preferred_element_type=jnp.float32
    )
    for h in range(H):
        d_stage[h] = delta[h : h + 1, :]
    d_slot[0] = d_stage[i]
    for r in range(1, H):
        to = there(r)
        remote(d_stage.at[to[1]], d_slot.at[r], d_send, d_recv, to)

    def arrived(a, g):
        dst = s1[a][1]
        if g == 0:
            wait_for(dst.at[pl.ds(PLACE[0] * G, T), :], s1_loc.at[a])
            if G > T:
                wait_for(dst.at[pl.ds(PLACE[0] * G + T, G - T), :], s1_recv.at[a, g])
        else:
            wait_for(dst.at[part(0, g), :], s1_recv.at[a, g])

    def first(n, g):
        kv, qd = (kg, vg)[n], (qg, gg)[n]
        arrived(2 * n, g)
        remote(kv.at[part(0, g), :], kv.at[part(2, g), :], kv_send.at[n, 2, g], kv_recv.at[n, 2, g], zpart)
        remote(kv.at[part(0, g), :], kv.at[part(1, g), :], kv_send.at[n, 1, g], kv_recv.at[n, 1, g], sib)
        arrived(2 * n + 1, g)
        for t in (2, 1, 3):
            remote(qd.at[part(0, g), :], qd.at[part(t, g), :], qg_send.at[n, t - 1, g], qg_recv.at[n, t - 1, g], ring(t))

    def forward(n, g):
        kv = (kg, vg)[n]
        wait_for(kv.at[part(2, g), :], kv_recv.at[n, 2, g])
        remote(kv.at[part(2, g), :], kv.at[part(3, g), :], kv_send.at[n, 0, g], kv_recv.at[n, 0, g], sib)

    def complete(n, g):
        kv, qd = (kg, vg)[n], (qg, gg)[n]
        for t in (1, 3, 2):
            wait_for(qd.at[part(t, g), :], qg_recv.at[n, t - 1, g])
        wait_for(kv.at[part(1, g), :], kv_recv.at[n, 1, g])
        wait_for(kv.at[part(3, g), :], kv_recv.at[n, 0, g])

    def stats(*blocks):
        for gq, gk in blocks:
            for h in range(halves):
                kc = gk * halves + h
                ks = pl.ds(kc * TK, TK)
                s = dot(kg[ks, :], qg[group(gq), :], NT)
                m = jnp.max(s, axis=0, keepdims=True) * c_log
                e = jnp.exp2(s * c_log - m)
                e_s[ks, group(gq)] = e
                m_s[pl.ds(kc, 1), group(gq)] = m
                l_s[pl.ds(kc, 1), group(gq)] = jnp.sum(e, axis=0, keepdims=True)

    lane = lax.broadcasted_iota(jnp.int32, (1, 128), 1) // T

    def stats_send(g):
        m = m_s[:, group(g)]
        top = jnp.max(m, axis=0, keepdims=True)
        total = jnp.sum(l_s[:, group(g)] * jnp.exp2(m - top), axis=0, keepdims=True)
        st[g, :, pl.ds(0, B)] = top + jnp.log2(total)
        st[g, :, pl.ds(B, 128)] = sum(jnp.where(lane == j, d_slot[per * g + j], 0.0) for j in range(per))
        for t in (2, 1, 3):
            remote(st.at[g], st_in.at[t - 1, g], st_send.at[t - 1, g], st_recv.at[t - 1, g], ring(t))

    def lanes(s):
        return pl.ds(PLACE[s] * G, G)

    def stats_take(g):
        for t in (1, 3, 2):
            wait_for(st_in.at[t - 1, g], st_recv.at[t - 1, g])
        for s in range(4):
            parts = [st[g, :, lanes(s)]] + [st_in[t - 1, g, :, lanes((s - t) % 4)] for t in (1, 2, 3)]
            top = functools.reduce(jnp.maximum, parts)
            norm = top + jnp.log2(sum(jnp.exp2(p - top) for p in parts))
            f_s[:, part(s, g)] = jnp.exp2(m_s[:, part(s, g)] - norm)
            delta_rows = st[g, :, pl.ds(B, G)] if s == 0 else st_in[s - 1, g, :, pl.ds(B, G)]
            d_all[pl.ds(0, 1), part(s, g)] = delta_rows

    def transpose_keys(g):
        kt[:, group(g)] = kg[group(g), :].T

    a, b, c3, d = S1_ORDER
    for n, g in enumerate(S1_ORDER):
        first(0, g)
        if n:
            forward(0, S1_ORDER[n - 1])
        if VG_AT == n + 1:
            s1_sends((2, 3))
    complete(0, a)
    stats((a, a))
    forward(0, d)
    complete(0, b)
    stats((a, b), (b, a), (b, b))
    first(1, a)
    complete(0, c3)
    stats((a, c3), (b, c3), (c3, a), (c3, b), (c3, c3))
    first(1, b)
    complete(0, d)
    stats((a, d), (b, d), (c3, d))
    first(1, c3)
    wait_for(d_slot.at[pl.ds(1, H - 1)], d_recv)
    for g in (a, b, c3):
        stats_send(g)
    forward(1, a)
    first(1, d)
    stats((d, a), (d, b), (d, c3), (d, d))
    stats_send(d)
    for g in (b, c3, d):
        forward(1, g)
    for g in range(4):
        transpose_keys(g)
    for g in range(4):
        complete(1, g)

    seen = set()

    def block(gq, gk):
        start_q, start_k = (gq, "q") not in seen, (gk, "k") not in seen
        seen.update(((gq, "q"), (gk, "k")))
        gv = gg[group(gq), :]
        qv = qg[group(gq), :]
        dp = dot(vg[group(gk), :], gv, NT)
        p = jnp.concatenate(
            [
                e_s[pl.ds(gk * B + h * TK, TK), group(gq)] * f_s[pl.ds(gk * halves + h, 1), group(gq)]
                for h in range(halves)
            ],
            axis=0,
        )
        ds = (p * ((dp - d_all[pl.ds(0, 1), group(gq)]) * scale)).astype(jnp.bfloat16)
        dv = dot(p.astype(jnp.bfloat16), gv, NN)
        dk = dot(ds, qv, NN)
        dq = dot(kt[:, group(gk)], ds, NN)
        dv_s[group(gk), :] = dv if start_k else dv_s[group(gk), :] + dv
        dk_s[group(gk), :] = dk if start_k else dk_s[group(gk), :] + dk
        dqt[:, group(gq)] = dq if start_q else dqt[:, group(gq)] + dq

    outs = (dq_out, dk_out, dv_out)

    def send_back(a, g):
        for j in range(per):
            r = g * per + j
            here = fin.at[a, pl.ds(r * T, T), :]
            if r == 0:
                pltpu.make_async_copy(here, outs[a].at[:, cols(i)], out_loc.at[a]).start()
            else:
                remote(here, outs[a].at[:, cols(i)], out_send.at[a], out_recv.at[a], back(r))

    sums = (dk_s, dv_s)

    def rows_of(g, first_row, count):
        return pl.ds(g * B + first_row * G, count * G)

    def to_sib(g):
        for j in range(2):
            sib_buf[g, j] = sums[j][rows_of(g, 0, 2), :].astype(jnp.bfloat16)
        remote(sib_buf.at[g], sib_in.at[g], sib_send.at[g], sib_recv.at[g], sib)

    def to_z(g):
        wait_for(sib_in.at[g], sib_recv.at[g])
        for j in range(2):
            t = sums[j][rows_of(g, 2, 1), :] + sib_in[g, j, pl.ds(0, G)].astype(jnp.float32)
            z_buf[g, j] = t.astype(jnp.bfloat16)
        remote(z_buf.at[g], z_in.at[g], z_send.at[g], z_recv.at[g], zpart)

    def to_owner(g):
        wait_for(z_in.at[g], z_recv.at[g])
        for j in range(2):
            t = sums[j][rows_of(g, 3, 1), :] + sib_in[g, j, pl.ds(G, G)].astype(jnp.float32)
            fin[1 + j, pl.ds(g * G, G), :] = (t + z_in[g, j].astype(jnp.float32)).astype(jnp.bfloat16)
        send_back(1, g)
        send_back(2, g)

    def dq_send_parts(g):
        for s in (2, 1, 3):
            dqb[s - 1, g] = dqt[:, part(s, g)].T.astype(jnp.bfloat16)
            remote(
                dqb.at[s - 1, g], dq_in.at[s - 1, g], dq_send.at[s - 1, g], dq_recv.at[s - 1, g], ring(4 - s)
            )

    def dq_owner(g):
        dq = dqt[:, part(0, g)].T
        for s in (1, 3, 2):
            wait_for(dq_in.at[s - 1, g], dq_recv.at[s - 1, g])
            dq = dq + dq_in[s - 1, g].astype(jnp.float32)
        fin[0, pl.ds(g * G, G), :] = dq.astype(jnp.bfloat16)
        send_back(0, g)

    k1, k2, k3, k4 = (3, 1, 2, 0)
    soon = [g for g in (k1, k2, k3, k4) if g != d] + [d]
    for g in soon:
        stats_take(g)
        block(g, k1)
    to_sib(k1)
    block(k1, k2)
    block(k1, k3)
    to_z(k1)
    block(k1, k4)
    dq_send_parts(k1)
    block(k2, k2)
    block(k3, k2)
    block(k4, k2)
    to_sib(k2)
    block(k2, k3)
    block(k2, k4)
    to_z(k2)
    dq_send_parts(k2)
    to_owner(k1)
    block(k3, k3)
    block(k4, k3)
    to_sib(k3)
    dq_owner(k1)
    block(k3, k4)
    to_z(k3)
    dq_send_parts(k3)
    block(k4, k4)
    to_sib(k4)
    dq_send_parts(k4)
    dq_owner(k2)
    to_z(k4)
    to_owner(k2)
    dq_owner(k3)
    to_owner(k3)
    dq_owner(k4)
    to_owner(k4)

    for a in range(4):
        wait_for(qg.at[pl.ds(T, B - T), :], s1_send.at[a])
    wait_for(d_slot.at[pl.ds(1, H - 1)], d_send)
    for n in range(2):
        for s in range(3):
            for g in range(4):
                wait_for(kg.at[part(0, g), :], kv_send.at[n, s, g])
                wait_for(qg.at[part(0, g), :], qg_send.at[n, s, g])
    for g in range(4):
        for t in range(3):
            wait_for(st.at[g], st_send.at[t, g])
            wait_for(dqb.at[t, g], dq_send.at[t, g])
        wait_for(sib_buf.at[g], sib_send.at[g])
        wait_for(z_buf.at[g], z_send.at[g])
    for a in (1, 2, 0):
        wait_for(fin.at[a, pl.ds(T, B - T), :], out_send.at[a])
        wait_for(fin.at[a, pl.ds(0, T), :], out_loc.at[a])
        wait_for(fin.at[a, pl.ds(T, B - T), :], out_recv.at[a])


def hand_over(a_in, b_in, c_in, a_out, b_out, c_out):
    a_out[...] = a_in[...]
    b_out[...] = b_in[...]
    c_out[...] = c_in[...]


def attention_backward(nx, outer, inner, queries, keys, values, outputs, out_grads):
    T, W = queries.shape
    D = HEAD_DIM
    H = inner
    B = H * T
    NQ = 4 * B
    TK = min(256, B)
    bf, f32 = jnp.bfloat16, jnp.float32
    dma = pltpu.SemaphoreType.DMA
    vm = pltpu.VMEM
    hbm = pl.BlockSpec(memory_space=pltpu.HBM)
    grads = pl.pallas_call(
        functools.partial(kernel, (H, nx, outer // 4, T, TK)),
        out_shape=[jax.ShapeDtypeStruct((T, W), bf)] * 3,
        in_specs=[hbm] * 5,
        out_specs=[hbm] * 3,
        scratch_shapes=[
            vm((NQ, D), bf), vm((NQ, D), bf), vm((NQ, D), bf), vm((NQ, D), bf),
            vm((D, NQ), bf),
            vm((NQ, NQ), f32),
            vm((NQ // TK, NQ), f32), vm((NQ // TK, NQ), f32), vm((NQ // TK, NQ), f32),
            vm((T, W), bf), vm((T, W), bf),
            vm((H, 1, 128), f32), vm((H, 1, 128), f32),
            vm((8, NQ), f32),
            vm((4, 1, B + 128), f32), vm((3, 4, 1, B + 128), f32),
            vm((D, NQ), f32),
            vm((NQ, D), f32), vm((NQ, D), f32),
            vm((4, 2, B // 2, D), bf), vm((4, 2, B // 2, D), bf),
            vm((4, 2, B // 4, D), bf), vm((4, 2, B // 4, D), bf),
            vm((3, 4, B // 4, D), bf), vm((3, 4, B // 4, D), bf),
            vm((3, B, D), bf),
            dma((2,)), dma((4,)), dma((4, 4)), dma((4,)), dma, dma,
            dma((2, 3, 4)), dma((2, 3, 4)), dma((2, 3, 4)), dma((2, 3, 4)), dma((3, 4)), dma((3, 4)),
            dma((4,)), dma((4,)), dma((4,)), dma((4,)), dma((3, 4)), dma((3, 4)), dma((3,)), dma((3,)), dma((3,)),
        ],
        compiler_params=pltpu.CompilerParams(
            collective_id=0, has_side_effects=True, vmem_limit_bytes=VMEM_LIMIT
        ),
        cost_estimate=pl.CostEstimate(flops=6 * 10**9, bytes_accessed=10**6, transcendentals=4 * 10**6),
    )(queries, keys, values, outputs, out_grads)
    vmem = pl.BlockSpec(memory_space=pltpu.VMEM)
    return pl.pallas_call(
        hand_over,
        out_shape=[jax.ShapeDtypeStruct((T, W), bf)] * 3,
        in_specs=[vmem] * 3,
        out_specs=[vmem] * 3,
    )(*grads)


def solution(mesh, nx=4):
    spec = P(("outer", "inner"), None)
    return jax.shard_map(
        functools.partial(attention_backward, nx, mesh.shape["outer"], mesh.shape["inner"]),
        mesh=mesh,
        in_specs=(spec,) * 5,
        out_specs=(spec,) * 3,
        check_vma=False,
    )
```

```python
import functools

import jax
import jax.numpy as jnp
import numpy as np
from jax import lax
from jax.experimental import pallas as pl
from jax.experimental.pallas import tpu as pltpu
from jax.sharding import PartitionSpec as P

HEAD_DIM = 128
MESH = pl.DeviceIdType.MESH
NT = (((1,), (1,)), ((), ()))
NN = (((1,), (0,)), ((), ()))
LOG2E = float(np.log2(np.e))
S1_ORDER = (0, 2, 1, 3)
VMEM_LIMIT = 62 << 20
VG_AT = 3
AHEAD = 2


def dot(a, b, dims):
    return lax.dot_general(a, b, dims, preferred_element_type=jnp.float32)


def kernel(
    cfg,
    q_in, k_in, v_in, o_in, g_in,
    out,
    qg, kg, vg, gg, kt, e_s, m_s, l_s, f_s,
    own_o, own_g, d_stage, d_slot, d_all, st, st_in, dqt, dk_s, dv_s, dp_s, sib_buf, sib_in, z_buf, z_in, dqb, dq_in, fin,
    in_sem, s1_send, s1_recv, s1_loc, d_send, d_recv,
    kv_send, kv_recv, qg_send, qg_recv, st_send, st_recv,
    sib_send, sib_recv, z_send, z_recv, dq_send, dq_recv, out_send, out_recv, out_loc,
):
    H, NX, NY, T, TK = cfg
    NZ = 2 * (H // NX)
    D = HEAD_DIM
    B = H * T
    G = B // 4
    per = H // 4
    scale = D ** (-0.5)
    c_log = scale * LOG2E
    halves = B // TK

    o = lax.axis_index("outer")
    i = lax.axis_index("inner")
    c = lax.rem(o, 2)
    y = lax.rem(lax.div(o, 2), NY)
    zl = lax.div(o, 2 * NY)
    x = lax.rem(i, NX)
    z = 2 * lax.div(i, NX) + zl
    up = 2 * zl - 1

    def dev(z_, y_, c_, x_):
        return ((lax.rem(z_, 2) * NY + y_) * 2 + c_, lax.div(z_, 2) * NX + x_)

    def along(dz, dx):
        return dev(lax.rem(z + dz + NZ, NZ), y, c, lax.rem(x + dx, NX))

    def there(r):
        g, dx = r // NX, r % NX
        return along((0, -2 * up, up, 3 * up)[g], dx)

    def back(r):
        g, dx = r // NX, r % NX
        return along((0, 2 * up, up, 3 * up)[g], NX - dx)

    sib = dev(z, y, 1 - c, x)
    zpart = dev(z - up, y, c, x)

    def ring(t):
        return dev(z, lax.rem(y + t, NY), c, x)

    def remote(src, dst, ssem, rsem, device):
        pltpu.make_async_remote_copy(
            src_ref=src, dst_ref=dst, send_sem=ssem, recv_sem=rsem, device_id=device, device_id_type=MESH
        ).start()

    def wait_for(ref, sem):
        pltpu.make_async_copy(ref, ref, sem).wait()

    def cols(h):
        return pl.ds(pl.multiple_of(h * D, D), D)

    cp_g = pltpu.make_async_copy(g_in, own_g, in_sem.at[0])
    cp_o = pltpu.make_async_copy(o_in, own_o, in_sem.at[1])
    cp_g.start()
    cp_o.start()

    barrier = pltpu.get_barrier_semaphore()
    partners = [there(r) for r in range(H - 1, 0, -1)] + [back(NX + dx) for dx in range(NX)]
    partners += [ring(2), ring(1), ring(3), zpart, sib]
    for p in partners:
        pl.semaphore_signal(barrier, inc=1, device_id=p, device_id_type=MESH)

    pl.semaphore_wait(barrier, len(partners))

    PLACE = (3, 1, 2, 0)

    def part(s, g):
        return pl.ds(g * B + PLACE[s] * G, G)

    def group(g):
        return pl.ds(g * B, B)

    s1 = ((k_in, kg), (q_in, qg), (v_in, vg), (g_in, gg))

    def s1_sends(pair):
        for a in pair:
            src, dst = s1[a]
            pltpu.make_async_copy(src.at[:, cols(i)], dst.at[pl.ds(PLACE[0] * G, T), :], s1_loc.at[a]).start()
        for g in S1_ORDER:
            for j in range(per):
                r = g * per + j
                if r == 0:
                    continue
                to = there(r)
                for a in pair:
                    src, dst = s1[a]
                    remote(
                        src.at[:, cols(to[1])],
                        dst.at[pl.ds(g * B + PLACE[0] * G + j * T, T), :],
                        s1_send.at[a],
                        s1_recv.at[a, g],
                        to,
                    )

    s1_sends((0, 1))

    cp_g.wait()
    cp_o.wait()
    prod = own_g[...].astype(jnp.float32) * own_o[...].astype(jnp.float32)
    prod4 = jnp.concatenate([prod] * 4, axis=0)
    pick = (
        lax.broadcasted_iota(jnp.int32, (H, H * D), 0) == lax.broadcasted_iota(jnp.int32, (H, H * D), 1) // D
    ).astype(jnp.float32)
    delta = lax.dot_general(
        pick, prod4, NT, precision=lax.Precision.HIGHEST, preferred_element_type=jnp.float32
    )
    for h in range(H):
        d_stage[h] = delta[h : h + 1, :]
    d_slot[0] = d_stage[i]
    for r in range(1, H):
        to = there(r)
        remote(d_stage.at[to[1]], d_slot.at[r], d_send, d_recv, to)

    def arrived(a, g):
        dst = s1[a][1]
        if g == 0:
            wait_for(dst.at[pl.ds(PLACE[0] * G, T), :], s1_loc.at[a])
            if G > T:
                wait_for(dst.at[pl.ds(PLACE[0] * G + T, G - T), :], s1_recv.at[a, g])
        else:
            wait_for(dst.at[part(0, g), :], s1_recv.at[a, g])

    def first(n, g):
        kv, qd = (kg, vg)[n], (qg, gg)[n]
        arrived(2 * n, g)
        remote(kv.at[part(0, g), :], kv.at[part(2, g), :], kv_send.at[n, 2, g], kv_recv.at[n, 2, g], zpart)
        remote(kv.at[part(0, g), :], kv.at[part(1, g), :], kv_send.at[n, 1, g], kv_recv.at[n, 1, g], sib)
        arrived(2 * n + 1, g)
        for t in (2, 1, 3):
            remote(qd.at[part(0, g), :], qd.at[part(t, g), :], qg_send.at[n, t - 1, g], qg_recv.at[n, t - 1, g], ring(t))

    def forward(n, g):
        kv = (kg, vg)[n]
        wait_for(kv.at[part(2, g), :], kv_recv.at[n, 2, g])
        remote(kv.at[part(2, g), :], kv.at[part(3, g), :], kv_send.at[n, 0, g], kv_recv.at[n, 0, g], sib)

    def complete(n, g):
        kv, qd = (kg, vg)[n], (qg, gg)[n]
        for t in (1, 3, 2):
            wait_for(qd.at[part(t, g), :], qg_recv.at[n, t - 1, g])
        wait_for(kv.at[part(1, g), :], kv_recv.at[n, 1, g])
        wait_for(kv.at[part(3, g), :], kv_recv.at[n, 0, g])

    def stats(*blocks):
        for gq, gk in blocks:
            for h in range(halves):
                kc = gk * halves + h
                ks = pl.ds(kc * TK, TK)
                s = dot(kg[ks, :], qg[group(gq), :], NT)
                m = jnp.max(s, axis=0, keepdims=True) * c_log
                e = jnp.exp2(s * c_log - m)
                e_s[ks, group(gq)] = e
                m_s[pl.ds(kc, 1), group(gq)] = m
                l_s[pl.ds(kc, 1), group(gq)] = jnp.sum(e, axis=0, keepdims=True)

    lane = lax.broadcasted_iota(jnp.int32, (1, 128), 1) // T

    def stats_send(g):
        m = m_s[:, group(g)]
        top = jnp.max(m, axis=0, keepdims=True)
        total = jnp.sum(l_s[:, group(g)] * jnp.exp2(m - top), axis=0, keepdims=True)
        st[g, :, pl.ds(0, B)] = top + jnp.log2(total)
        st[g, :, pl.ds(B, 128)] = sum(jnp.where(lane == j, d_slot[per * g + j], 0.0) for j in range(per))
        for t in (2, 1, 3):
            remote(st.at[g], st_in.at[t - 1, g], st_send.at[t - 1, g], st_recv.at[t - 1, g], ring(t))

    def lanes(s):
        return pl.ds(PLACE[s] * G, G)

    def stats_take(g):
        for t in (1, 3, 2):
            wait_for(st_in.at[t - 1, g], st_recv.at[t - 1, g])
        for s in range(4):
            parts = [st[g, :, lanes(s)]] + [st_in[t - 1, g, :, lanes((s - t) % 4)] for t in (1, 2, 3)]
            top = functools.reduce(jnp.maximum, parts)
            norm = top + jnp.log2(sum(jnp.exp2(p - top) for p in parts))
            f_s[:, part(s, g)] = jnp.exp2(m_s[:, part(s, g)] - norm)
            delta_rows = st[g, :, pl.ds(B, G)] if s == 0 else st_in[s - 1, g, :, pl.ds(B, G)]
            d_all[pl.ds(0, 1), part(s, g)] = delta_rows

    def transpose_keys(g):
        kt[:, group(g)] = kg[group(g), :].T

    a, b, c3, d = S1_ORDER
    for n, g in enumerate(S1_ORDER):
        first(0, g)
        if n:
            forward(0, S1_ORDER[n - 1])
        if VG_AT == n + 1:
            s1_sends((2, 3))
    complete(0, a)
    stats((a, a))
    forward(0, d)
    complete(0, b)
    stats((a, b), (b, a), (b, b))
    first(1, a)
    complete(0, c3)
    stats((a, c3), (b, c3), (c3, a), (c3, b), (c3, c3))
    first(1, b)
    complete(0, d)
    stats((a, d), (b, d), (c3, d))
    first(1, c3)
    wait_for(d_slot.at[pl.ds(1, H - 1)], d_recv)
    for g in (a, b, c3):
        stats_send(g)
    forward(1, a)
    first(1, d)
    stats((d, a), (d, b), (d, c3), (d, d))
    stats_send(d)
    for g in (b, c3, d):
        forward(1, g)
    for g in range(4):
        transpose_keys(g)
    ahead = {}
    for n in range(AHEAD):
        complete(1, S1_ORDER[n])
        new = [(S1_ORDER[n], S1_ORDER[j]) for j in range(n + 1)] + [(S1_ORDER[j], S1_ORDER[n]) for j in range(n)]
        for gq, gk in new:
            ahead[gq, gk] = len(ahead)
            dp_s[ahead[gq, gk]] = dot(vg[group(gk), :], gg[group(gq), :], NT)
    for n in range(AHEAD, 4):
        complete(1, S1_ORDER[n])

    seen = set()

    def block(gq, gk):
        start_q, start_k = (gq, "q") not in seen, (gk, "k") not in seen
        seen.update(((gq, "q"), (gk, "k")))
        gv = gg[group(gq), :]
        qv = qg[group(gq), :]
        dp = dp_s[ahead[gq, gk]] if (gq, gk) in ahead else dot(vg[group(gk), :], gv, NT)
        p = jnp.concatenate(
            [
                e_s[pl.ds(gk * B + h * TK, TK), group(gq)] * f_s[pl.ds(gk * halves + h, 1), group(gq)]
                for h in range(halves)
            ],
            axis=0,
        )
        ds = (p * ((dp - d_all[pl.ds(0, 1), group(gq)]) * scale)).astype(jnp.bfloat16)
        dv = dot(p.astype(jnp.bfloat16), gv, NN)
        dk = dot(ds, qv, NN)
        dq = dot(kt[:, group(gk)], ds, NN)
        dv_s[group(gk), :] = dv if start_k else dv_s[group(gk), :] + dv
        dk_s[group(gk), :] = dk if start_k else dk_s[group(gk), :] + dk
        dqt[:, group(gq)] = dq if start_q else dqt[:, group(gq)] + dq

    def send_back(n, g):
        pick = pl.ds(n, n + 1)
        for j in range(per):
            r = g * per + j
            here = fin.at[pick, pl.ds(r * T, T), :]
            if r == 0:
                pltpu.make_async_copy(here, out.at[pick, :, cols(i)], out_loc.at[n]).start()
            else:
                remote(here, out.at[pick, :, cols(i)], out_send.at[n], out_recv.at[n], back(r))

    sums = (dk_s, dv_s)

    def rows_of(g, first_row, count):
        return pl.ds(g * B + first_row * G, count * G)

    def to_sib(g):
        for j in range(2):
            sib_buf[g, j] = sums[j][rows_of(g, 0, 2), :].astype(jnp.bfloat16)
        remote(sib_buf.at[g], sib_in.at[g], sib_send.at[g], sib_recv.at[g], sib)

    def to_z(g):
        wait_for(sib_in.at[g], sib_recv.at[g])
        for j in range(2):
            t = sums[j][rows_of(g, 2, 1), :] + sib_in[g, j, pl.ds(0, G)].astype(jnp.float32)
            z_buf[g, j] = t.astype(jnp.bfloat16)
        remote(z_buf.at[g], z_in.at[g], z_send.at[g], z_recv.at[g], zpart)

    def to_owner(g):
        wait_for(z_in.at[g], z_recv.at[g])
        for j in range(2):
            t = sums[j][rows_of(g, 3, 1), :] + sib_in[g, j, pl.ds(G, G)].astype(jnp.float32)
            fin[1 + j, pl.ds(g * G, G), :] = (t + z_in[g, j].astype(jnp.float32)).astype(jnp.bfloat16)
        send_back(1, g)

    def dq_send_parts(g):
        for s in (2, 1, 3):
            dqb[s - 1, g] = dqt[:, part(s, g)].astype(jnp.bfloat16).T
            remote(
                dqb.at[s - 1, g], dq_in.at[s - 1, g], dq_send.at[s - 1, g], dq_recv.at[s - 1, g], ring(4 - s)
            )

    def dq_owner(g):
        dq = dqt[:, part(0, g)].T
        for s in (1, 3, 2):
            wait_for(dq_in.at[s - 1, g], dq_recv.at[s - 1, g])
            dq = dq + dq_in[s - 1, g].astype(jnp.float32)
        fin[0, pl.ds(g * G, G), :] = dq.astype(jnp.bfloat16)
        send_back(0, g)

    k1, k2, k3, k4 = (3, 1, 2, 0)
    soon = [g for g in (k1, k2, k3, k4) if g != d] + [d]
    for g in soon:
        stats_take(g)
        block(g, k1)
    to_sib(k1)
    block(k1, k2)
    block(k1, k3)
    to_z(k1)
    block(k1, k4)
    dq_send_parts(k1)
    block(k2, k2)
    block(k3, k2)
    block(k4, k2)
    to_sib(k2)
    block(k2, k3)
    block(k2, k4)
    to_z(k2)
    dq_send_parts(k2)
    to_owner(k1)
    block(k3, k3)
    block(k4, k3)
    to_sib(k3)
    dq_owner(k1)
    block(k3, k4)
    dq_send_parts(k3)
    to_z(k3)
    block(k4, k4)
    to_sib(k4)
    dq_send_parts(k4)
    dq_owner(k2)
    to_z(k4)
    to_owner(k2)
    dq_owner(k3)
    to_owner(k3)
    dq_owner(k4)
    to_owner(k4)

    for a in range(4):
        wait_for(qg.at[pl.ds(T, B - T), :], s1_send.at[a])
    wait_for(d_slot.at[pl.ds(1, H - 1)], d_send)
    for n in range(2):
        for s in range(3):
            for g in range(4):
                wait_for(kg.at[part(0, g), :], kv_send.at[n, s, g])
                wait_for(qg.at[part(0, g), :], qg_send.at[n, s, g])
    for g in range(4):
        for t in range(3):
            wait_for(st.at[g], st_send.at[t, g])
            wait_for(dqb.at[t, g], dq_send.at[t, g])
        wait_for(sib_buf.at[g], sib_send.at[g])
        wait_for(z_buf.at[g], z_send.at[g])
    for n in (1, 0):
        pick = pl.ds(n, n + 1)
        wait_for(fin.at[pick, pl.ds(T, B - T), :], out_send.at[n])
        wait_for(fin.at[pick, pl.ds(0, T), :], out_loc.at[n])
        wait_for(fin.at[pick, pl.ds(T, B - T), :], out_recv.at[n])


def hand_over(grads, dq_out, dk_out, dv_out):
    dq_out[...] = grads[0]
    dk_out[...] = grads[1]
    dv_out[...] = grads[2]


def attention_backward(nx, outer, inner, queries, keys, values, outputs, out_grads):
    T, W = queries.shape
    D = HEAD_DIM
    H = inner
    B = H * T
    NQ = 4 * B
    TK = min(256, B)
    bf, f32 = jnp.bfloat16, jnp.float32
    dma = pltpu.SemaphoreType.DMA
    vm = pltpu.VMEM
    hbm = pl.BlockSpec(memory_space=pltpu.HBM)
    grads = pl.pallas_call(
        functools.partial(kernel, (H, nx, outer // 4, T, TK)),
        out_shape=jax.ShapeDtypeStruct((3, T, W), bf),
        in_specs=[hbm] * 5,
        out_specs=hbm,
        scratch_shapes=[
            vm((NQ, D), bf), vm((NQ, D), bf), vm((NQ, D), bf), vm((NQ, D), bf),
            vm((D, NQ), bf),
            vm((NQ, NQ), f32),
            vm((NQ // TK, NQ), f32), vm((NQ // TK, NQ), f32), vm((NQ // TK, NQ), f32),
            vm((T, W), bf), vm((T, W), bf),
            vm((H, 1, 128), f32), vm((H, 1, 128), f32),
            vm((8, NQ), f32),
            vm((4, 1, B + 128), f32), vm((3, 4, 1, B + 128), f32),
            vm((D, NQ), f32),
            vm((NQ, D), f32), vm((NQ, D), f32),
            vm((max(AHEAD * AHEAD, 1), B, B), f32),
            vm((4, 2, B // 2, D), bf), vm((4, 2, B // 2, D), bf),
            vm((4, 2, B // 4, D), bf), vm((4, 2, B // 4, D), bf),
            vm((3, 4, B // 4, D), bf), vm((3, 4, B // 4, D), bf),
            vm((3, B, D), bf),
            dma((2,)), dma((4,)), dma((4, 4)), dma((4,)), dma, dma,
            dma((2, 3, 4)), dma((2, 3, 4)), dma((2, 3, 4)), dma((2, 3, 4)), dma((3, 4)), dma((3, 4)),
            dma((4,)), dma((4,)), dma((4,)), dma((4,)), dma((3, 4)), dma((3, 4)), dma((2,)), dma((2,)), dma((2,)),
        ],
        compiler_params=pltpu.CompilerParams(
            collective_id=0, has_side_effects=True, vmem_limit_bytes=VMEM_LIMIT
        ),
        cost_estimate=pl.CostEstimate(flops=6 * 10**9, bytes_accessed=10**6, transcendentals=4 * 10**6),
    )(queries, keys, values, outputs, out_grads)
    vmem = pl.BlockSpec(memory_space=pltpu.VMEM)
    return pl.pallas_call(
        hand_over,
        out_shape=[jax.ShapeDtypeStruct((T, W), bf)] * 3,
        in_specs=[vmem],
        out_specs=[vmem] * 3,
    )(grads)


def solution(mesh, nx=4):
    spec = P(("outer", "inner"), None)
    return jax.shard_map(
        functools.partial(attention_backward, nx, mesh.shape["outer"], mesh.shape["inner"]),
        mesh=mesh,
        in_specs=(spec,) * 5,
        out_specs=(spec,) * 3,
        check_vma=False,
    )
```

```python
import functools

import jax
import jax.numpy as jnp
import numpy as np
from jax import lax
from jax.experimental import pallas as pl
from jax.experimental.pallas import tpu as pltpu
from jax.sharding import PartitionSpec as P

HEAD_DIM = 128
MESH = pl.DeviceIdType.MESH
NT = (((1,), (1,)), ((), ()))
NN = (((1,), (0,)), ((), ()))
LOG2E = float(np.log2(np.e))
S1_ORDER = (0, 2, 1, 3)
VMEM_LIMIT = 62 << 20
VG_AT = 3
AHEAD = 2


def dot(a, b, dims):
    return lax.dot_general(a, b, dims, preferred_element_type=jnp.float32)


def kernel(
    cfg,
    q_in, k_in, v_in, o_in, g_in,
    out,
    qg, kg, vg, gg, kt, e_s, m_s, l_s, f_s,
    own_o, own_g, d_stage, d_slot, d_all, st, st_in, dqt, dk_s, dv_s, dp_s, sib_buf, sib_in, z_buf, z_in, dqb, dq_in, fin,
    in_sem, s1_send, s1_recv, s1_loc, d_send, d_recv,
    kv_send, kv_recv, qg_send, qg_recv, st_send, st_recv,
    sib_send, sib_recv, z_send, z_recv, dq_send, dq_recv, out_send, out_recv, out_loc,
):
    H, NX, NY, T, TK = cfg
    NZ = 2 * (H // NX)
    D = HEAD_DIM
    B = H * T
    G = B // 4
    per = H // 4
    scale = D ** (-0.5)
    c_log = scale * LOG2E
    halves = B // TK

    o = lax.axis_index("outer")
    i = lax.axis_index("inner")
    c = lax.rem(o, 2)
    y = lax.rem(lax.div(o, 2), NY)
    zl = lax.div(o, 2 * NY)
    x = lax.rem(i, NX)
    z = 2 * lax.div(i, NX) + zl
    up = 2 * zl - 1

    def dev(z_, y_, c_, x_):
        return ((lax.rem(z_, 2) * NY + y_) * 2 + c_, lax.div(z_, 2) * NX + x_)

    def along(dz, dx):
        return dev(lax.rem(z + dz + NZ, NZ), y, c, lax.rem(x + dx, NX))

    def there(r):
        g, dx = r // NX, r % NX
        return along((0, -2 * up, up, 3 * up)[g], dx)

    def back(r):
        g, dx = r // NX, r % NX
        return along((0, 2 * up, up, 3 * up)[g], NX - dx)

    sib = dev(z, y, 1 - c, x)
    zpart = dev(z - up, y, c, x)

    def ring(t):
        return dev(z, lax.rem(y + t, NY), c, x)

    def remote(src, dst, ssem, rsem, device):
        pltpu.make_async_remote_copy(
            src_ref=src, dst_ref=dst, send_sem=ssem, recv_sem=rsem, device_id=device, device_id_type=MESH
        ).start()

    def wait_for(ref, sem):
        pltpu.make_async_copy(ref, ref, sem).wait()

    def cols(h):
        return pl.ds(pl.multiple_of(h * D, D), D)

    cp_g = pltpu.make_async_copy(g_in, own_g, in_sem.at[0])
    cp_o = pltpu.make_async_copy(o_in, own_o, in_sem.at[1])
    cp_g.start()
    cp_o.start()

    barrier = pltpu.get_barrier_semaphore()
    partners = [there(r) for r in range(H - 1, 0, -1)] + [back(NX + dx) for dx in range(NX)]
    partners += [ring(2), ring(1), ring(3), zpart, sib]
    for p in partners:
        pl.semaphore_signal(barrier, inc=1, device_id=p, device_id_type=MESH)

    pl.semaphore_wait(barrier, len(partners))

    PLACE = (3, 1, 2, 0)

    def part(s, g):
        return pl.ds(g * B + PLACE[s] * G, G)

    def group(g):
        return pl.ds(g * B, B)

    s1 = ((k_in, kg), (q_in, qg), (v_in, vg), (g_in, gg))

    def s1_sends(pair):
        for a in pair:
            src, dst = s1[a]
            pltpu.make_async_copy(src.at[:, cols(i)], dst.at[pl.ds(PLACE[0] * G, T), :], s1_loc.at[a]).start()
        for g in S1_ORDER:
            for j in range(per):
                r = g * per + j
                if r == 0:
                    continue
                to = there(r)
                for a in pair:
                    src, dst = s1[a]
                    remote(
                        src.at[:, cols(to[1])],
                        dst.at[pl.ds(g * B + PLACE[0] * G + j * T, T), :],
                        s1_send.at[a],
                        s1_recv.at[a, g],
                        to,
                    )

    s1_sends((0, 1))

    cp_g.wait()
    cp_o.wait()
    prod = own_g[...].astype(jnp.float32) * own_o[...].astype(jnp.float32)
    prod4 = jnp.concatenate([prod] * 4, axis=0)
    pick = (
        lax.broadcasted_iota(jnp.int32, (H, H * D), 0) == lax.broadcasted_iota(jnp.int32, (H, H * D), 1) // D
    ).astype(jnp.float32)
    delta = lax.dot_general(
        pick, prod4, NT, precision=lax.Precision.HIGHEST, preferred_element_type=jnp.float32
    )
    for h in range(H):
        d_stage[h] = delta[h : h + 1, :]
    d_slot[0] = d_stage[i]
    for r in range(1, H):
        to = there(r)
        remote(d_stage.at[to[1]], d_slot.at[r], d_send, d_recv, to)

    def arrived(a, g):
        dst = s1[a][1]
        if g == 0:
            wait_for(dst.at[pl.ds(PLACE[0] * G, T), :], s1_loc.at[a])
            if G > T:
                wait_for(dst.at[pl.ds(PLACE[0] * G + T, G - T), :], s1_recv.at[a, g])
        else:
            wait_for(dst.at[part(0, g), :], s1_recv.at[a, g])

    def first(n, g):
        kv, qd = (kg, vg)[n], (qg, gg)[n]
        arrived(2 * n, g)
        remote(kv.at[part(0, g), :], kv.at[part(2, g), :], kv_send.at[n, 2, g], kv_recv.at[n, 2, g], zpart)
        remote(kv.at[part(0, g), :], kv.at[part(1, g), :], kv_send.at[n, 1, g], kv_recv.at[n, 1, g], sib)
        arrived(2 * n + 1, g)
        for t in (2, 1, 3):
            remote(qd.at[part(0, g), :], qd.at[part(t, g), :], qg_send.at[n, t - 1, g], qg_recv.at[n, t - 1, g], ring(t))

    def forward(n, g):
        kv = (kg, vg)[n]
        wait_for(kv.at[part(2, g), :], kv_recv.at[n, 2, g])
        remote(kv.at[part(2, g), :], kv.at[part(3, g), :], kv_send.at[n, 0, g], kv_recv.at[n, 0, g], sib)

    def complete(n, g):
        kv, qd = (kg, vg)[n], (qg, gg)[n]
        for t in (1, 3, 2):
            wait_for(qd.at[part(t, g), :], qg_recv.at[n, t - 1, g])
        wait_for(kv.at[part(1, g), :], kv_recv.at[n, 1, g])
        wait_for(kv.at[part(3, g), :], kv_recv.at[n, 0, g])

    def stats(*blocks):
        for gq, gk in blocks:
            for h in range(halves):
                kc = gk * halves + h
                ks = pl.ds(kc * TK, TK)
                s = dot(kg[ks, :], qg[group(gq), :], NT)
                m = jnp.max(s, axis=0, keepdims=True) * c_log
                e = jnp.exp2(s * c_log - m)
                e_s[ks, group(gq)] = e
                m_s[pl.ds(kc, 1), group(gq)] = m
                l_s[pl.ds(kc, 1), group(gq)] = jnp.sum(e, axis=0, keepdims=True)

    lane = lax.broadcasted_iota(jnp.int32, (1, 128), 1) // T

    def stats_send(g):
        m = m_s[:, group(g)]
        top = jnp.max(m, axis=0, keepdims=True)
        total = jnp.sum(l_s[:, group(g)] * jnp.exp2(m - top), axis=0, keepdims=True)
        st[g, :, pl.ds(0, B)] = top + jnp.log2(total)
        st[g, :, pl.ds(B, 128)] = sum(jnp.where(lane == j, d_slot[per * g + j], 0.0) for j in range(per))
        for t in (2, 1, 3):
            remote(st.at[g], st_in.at[t - 1, g], st_send.at[t - 1, g], st_recv.at[t - 1, g], ring(t))

    def lanes(s):
        return pl.ds(PLACE[s] * G, G)

    def stats_take(g):
        for t in (1, 3, 2):
            wait_for(st_in.at[t - 1, g], st_recv.at[t - 1, g])
        for s in range(4):
            parts = [st[g, :, lanes(s)]] + [st_in[t - 1, g, :, lanes((s - t) % 4)] for t in (1, 2, 3)]
            top = functools.reduce(jnp.maximum, parts)
            norm = top + jnp.log2(sum(jnp.exp2(p - top) for p in parts))
            f_s[:, part(s, g)] = jnp.exp2(m_s[:, part(s, g)] - norm)
            delta_rows = st[g, :, pl.ds(B, G)] if s == 0 else st_in[s - 1, g, :, pl.ds(B, G)]
            d_all[pl.ds(0, 1), part(s, g)] = delta_rows

    def transpose_keys(g):
        kt[:, group(g)] = kg[group(g), :].T

    a, b, c3, d = S1_ORDER
    for n, g in enumerate(S1_ORDER):
        first(0, g)
        if n:
            forward(0, S1_ORDER[n - 1])
        if VG_AT == n + 1:
            s1_sends((2, 3))
    complete(0, a)
    stats((a, a))
    forward(0, d)
    complete(0, b)
    stats((a, b), (b, a), (b, b))
    first(1, a)
    complete(0, c3)
    stats((a, c3), (b, c3), (c3, a), (c3, b), (c3, c3))
    first(1, b)
    complete(0, d)
    stats((a, d), (b, d), (c3, d))
    first(1, c3)
    wait_for(d_slot.at[pl.ds(1, H - 1)], d_recv)
    for g in (a, b, c3):
        stats_send(g)
    forward(1, a)
    first(1, d)
    stats((d, a), (d, b), (d, c3), (d, d))
    stats_send(d)
    for g in (b, c3, d):
        forward(1, g)
    for g in range(4):
        transpose_keys(g)
    ahead = {}
    for n in range(AHEAD):
        complete(1, S1_ORDER[n])
        new = [(S1_ORDER[n], S1_ORDER[j]) for j in range(n + 1)] + [(S1_ORDER[j], S1_ORDER[n]) for j in range(n)]
        for gq, gk in new:
            ahead[gq, gk] = len(ahead)
            dp_s[ahead[gq, gk]] = dot(vg[group(gk), :], gg[group(gq), :], NT)
    for n in range(AHEAD, 4):
        complete(1, S1_ORDER[n])

    seen = set()

    def block(gq, gk):
        start_q, start_k = (gq, "q") not in seen, (gk, "k") not in seen
        seen.update(((gq, "q"), (gk, "k")))
        gv = gg[group(gq), :]
        qv = qg[group(gq), :]
        dp = dp_s[ahead[gq, gk]] if (gq, gk) in ahead else dot(vg[group(gk), :], gv, NT)
        p = jnp.concatenate(
            [
                e_s[pl.ds(gk * B + h * TK, TK), group(gq)] * f_s[pl.ds(gk * halves + h, 1), group(gq)]
                for h in range(halves)
            ],
            axis=0,
        )
        ds = (p * ((dp - d_all[pl.ds(0, 1), group(gq)]) * scale)).astype(jnp.bfloat16)
        dv = dot(p.astype(jnp.bfloat16), gv, NN)
        dk = dot(ds, qv, NN)
        dq = dot(kt[:, group(gk)], ds, NN)
        dv_s[group(gk), :] = dv if start_k else dv_s[group(gk), :] + dv
        dk_s[group(gk), :] = dk if start_k else dk_s[group(gk), :] + dk
        dqt[:, group(gq)] = dq if start_q else dqt[:, group(gq)] + dq

    def send_back(n, g):
        pick = pl.ds(n, n + 1)
        for j in range(per):
            r = g * per + j
            here = fin.at[pick, pl.ds(r * T, T), :]
            if r == 0:
                pltpu.make_async_copy(here, out.at[pick, :, cols(i)], out_loc.at[n]).start()
            else:
                remote(here, out.at[pick, :, cols(i)], out_send.at[n], out_recv.at[n], back(r))

    sums = (dk_s, dv_s)

    def rows_of(g, first_row, count):
        return pl.ds(g * B + first_row * G, count * G)

    def to_sib(g):
        for j in range(2):
            sib_buf[g, j] = sums[j][rows_of(g, 0, 2), :].astype(jnp.bfloat16)
        remote(sib_buf.at[g], sib_in.at[g], sib_send.at[g], sib_recv.at[g], sib)

    def to_z(g):
        wait_for(sib_in.at[g], sib_recv.at[g])
        for j in range(2):
            t = sums[j][rows_of(g, 2, 1), :] + sib_in[g, j, pl.ds(0, G)].astype(jnp.float32)
            z_buf[g, j] = t.astype(jnp.bfloat16)
        remote(z_buf.at[g], z_in.at[g], z_send.at[g], z_recv.at[g], zpart)

    def to_owner(g):
        wait_for(z_in.at[g], z_recv.at[g])
        for j in range(2):
            t = sums[j][rows_of(g, 3, 1), :] + sib_in[g, j, pl.ds(G, G)].astype(jnp.float32)
            fin[1 + j, pl.ds(g * G, G), :] = (t + z_in[g, j].astype(jnp.float32)).astype(jnp.bfloat16)
        send_back(1, g)

    def dq_send_parts(g):
        for s in (2, 1, 3):
            dqb[s - 1, g] = dqt[:, part(s, g)].astype(jnp.bfloat16).T
            remote(
                dqb.at[s - 1, g], dq_in.at[s - 1, g], dq_send.at[s - 1, g], dq_recv.at[s - 1, g], ring(4 - s)
            )

    def dq_owner(g):
        dq = dqt[:, part(0, g)].T
        for s in (1, 3, 2):
            wait_for(dq_in.at[s - 1, g], dq_recv.at[s - 1, g])
            dq = dq + dq_in[s - 1, g].astype(jnp.float32)
        fin[0, pl.ds(g * G, G), :] = dq.astype(jnp.bfloat16)
        send_back(0, g)

    k1, k2, k3, k4 = (3, 1, 2, 0)
    soon = [g for g in (k1, k2, k3, k4) if g != d] + [d]
    for g in soon:
        stats_take(g)
        block(g, k1)
    to_sib(k1)
    block(k1, k2)
    block(k1, k3)
    to_z(k1)
    block(k1, k4)
    dq_send_parts(k1)
    block(k2, k2)
    block(k3, k2)
    block(k4, k2)
    to_sib(k2)
    block(k2, k3)
    block(k2, k4)
    to_z(k2)
    dq_send_parts(k2)
    to_owner(k1)
    block(k3, k3)
    block(k4, k3)
    to_sib(k3)
    dq_owner(k1)
    block(k3, k4)
    dq_send_parts(k3)
    to_z(k3)
    block(k4, k4)
    to_sib(k4)
    dq_send_parts(k4)
    to_z(k4)
    dq_owner(k2)
    to_owner(k2)
    dq_owner(k3)
    to_owner(k3)
    dq_owner(k4)
    to_owner(k4)

    for a in range(4):
        wait_for(qg.at[pl.ds(T, B - T), :], s1_send.at[a])
    wait_for(d_slot.at[pl.ds(1, H - 1)], d_send)
    for n in range(2):
        for s in range(3):
            for g in range(4):
                wait_for(kg.at[part(0, g), :], kv_send.at[n, s, g])
                wait_for(qg.at[part(0, g), :], qg_send.at[n, s, g])
    for g in range(4):
        for t in range(3):
            wait_for(st.at[g], st_send.at[t, g])
            wait_for(dqb.at[t, g], dq_send.at[t, g])
        wait_for(sib_buf.at[g], sib_send.at[g])
        wait_for(z_buf.at[g], z_send.at[g])
    for n in (1, 0):
        pick = pl.ds(n, n + 1)
        wait_for(fin.at[pick, pl.ds(T, B - T), :], out_send.at[n])
        wait_for(fin.at[pick, pl.ds(0, T), :], out_loc.at[n])
        wait_for(fin.at[pick, pl.ds(T, B - T), :], out_recv.at[n])


def hand_over(grads, dq_out, dk_out, dv_out):
    dq_out[...] = grads[0]
    dk_out[...] = grads[1]
    dv_out[...] = grads[2]


def attention_backward(nx, outer, inner, queries, keys, values, outputs, out_grads):
    T, W = queries.shape
    D = HEAD_DIM
    H = inner
    B = H * T
    NQ = 4 * B
    TK = min(256, B)
    bf, f32 = jnp.bfloat16, jnp.float32
    dma = pltpu.SemaphoreType.DMA
    vm = pltpu.VMEM
    hbm = pl.BlockSpec(memory_space=pltpu.HBM)
    grads = pl.pallas_call(
        functools.partial(kernel, (H, nx, outer // 4, T, TK)),
        out_shape=jax.ShapeDtypeStruct((3, T, W), bf),
        in_specs=[hbm] * 5,
        out_specs=hbm,
        scratch_shapes=[
            vm((NQ, D), bf), vm((NQ, D), bf), vm((NQ, D), bf), vm((NQ, D), bf),
            vm((D, NQ), bf),
            vm((NQ, NQ), f32),
            vm((NQ // TK, NQ), f32), vm((NQ // TK, NQ), f32), vm((NQ // TK, NQ), f32),
            vm((T, W), bf), vm((T, W), bf),
            vm((H, 1, 128), f32), vm((H, 1, 128), f32),
            vm((8, NQ), f32),
            vm((4, 1, B + 128), f32), vm((3, 4, 1, B + 128), f32),
            vm((D, NQ), f32),
            vm((NQ, D), f32), vm((NQ, D), f32),
            vm((max(AHEAD * AHEAD, 1), B, B), f32),
            vm((4, 2, B // 2, D), bf), vm((4, 2, B // 2, D), bf),
            vm((4, 2, B // 4, D), bf), vm((4, 2, B // 4, D), bf),
            vm((3, 4, B // 4, D), bf), vm((3, 4, B // 4, D), bf),
            vm((3, B, D), bf),
            dma((2,)), dma((4,)), dma((4, 4)), dma((4,)), dma, dma,
            dma((2, 3, 4)), dma((2, 3, 4)), dma((2, 3, 4)), dma((2, 3, 4)), dma((3, 4)), dma((3, 4)),
            dma((4,)), dma((4,)), dma((4,)), dma((4,)), dma((3, 4)), dma((3, 4)), dma((2,)), dma((2,)), dma((2,)),
        ],
        compiler_params=pltpu.CompilerParams(
            collective_id=0, has_side_effects=True, vmem_limit_bytes=VMEM_LIMIT
        ),
        cost_estimate=pl.CostEstimate(flops=6 * 10**9, bytes_accessed=10**6, transcendentals=4 * 10**6),
    )(queries, keys, values, outputs, out_grads)
    vmem = pl.BlockSpec(memory_space=pltpu.VMEM)
    return pl.pallas_call(
        hand_over,
        out_shape=[jax.ShapeDtypeStruct((T, W), bf)] * 3,
        in_specs=[vmem],
        out_specs=[vmem] * 3,
    )(grads)


def solution(mesh, nx=4):
    spec = P(("outer", "inner"), None)
    return jax.shard_map(
        functools.partial(attention_backward, nx, mesh.shape["outer"], mesh.shape["inner"]),
        mesh=mesh,
        in_specs=(spec,) * 5,
        out_specs=(spec,) * 3,
        check_vma=False,
    )
```
